256 devices in a mesh: dp: 32 (over z, y), seq: 8 (over x, core).
Axes of the slice: x: 4, y: 4, z: 8, core: 2. Of those that a mesh axis runs over, the one named last changes fastest.
Arguments:
- queries: bfloat16 [32, 1024, 4096], P('dp', 'seq'), may hold values from -112 to 112
- keys: bfloat16 [32, 1024, 1024], P('dp', 'seq'), may hold values from -6 to 6
- values: bfloat16 [32, 1024, 1024], P('dp', 'seq'), may hold values from -5 to 5
- out_grad: bfloat16 [32, 1024, 4096], P('dp', 'seq'), may hold values from -0.119628906 to 0.119628906
- doc_blocks: int32 [32, 3], P('dp'), may hold values from 1 to 4, 8 in all within a row
- pad_count: int32 [32, 3], P('dp'), may hold values from 0 to 127
- partner: int32 [32, 3], P('dp'), may hold values from 0 to 95, as said below
Outputs:
- q_grad: bfloat16 [32, 1024, 4096], P('dp', 'seq')
- k_grad: bfloat16 [32, 1024, 1024], P('dp', 'seq')
- v_grad: bfloat16 [32, 1024, 1024], P('dp', 'seq')
The draws below stay inside these ranges and needn't reach their ends.
Inputs may be any that keep to these rules, and one draw needn't show every extreme that they name: Entries of partner form one cycle through all 96 pooled embeddings: each value occurs once and no entry names its own anchor.
All inputs are finite; a program needn't handle non-finite values.
Results may differ from the reference program's by a relative error of at most 0.011.
Values may be sent and summed in bfloat16 or wider, within the bound.
No kernel may reach another device: no remote copies, remote signals or barrier semaphores. Data moves between devices by JAX's collectives and lax.ppermute only.
A program may use at most 64 MiB of HBM per device.

```python
import math
import jax
import jax.numpy as jnp
import numpy as np
from jax import lax

HQ = 32
KVH = 8
HD = 128
BLOCK = 128
DOCS = 3
DQ = 4096
KVD = 1024
LEN = 1024
PACKS = 32
POOLED = 96


def shared_keys(key):
    return jnp.clip(jax.random.normal(key, (PACKS, LEN, KVH * HD), jnp.float32), -5.0, 5.0)


def draw_keys(key, part):
    base = shared_keys(key)
    return base.astype(jnp.bfloat16)


def draw_queries(key, part):
    key = jax.random.fold_in(key, 13)
    fresh = jnp.clip(jax.random.normal(key, (PACKS, LEN, HQ * HD), jnp.float32), -5.0, 5.0)
    return fresh.astype(jnp.bfloat16)


def draw_partner(key, part):
    key = jax.random.fold_in(key, 7)
    order = jax.random.permutation(key, PACKS * DOCS).astype(jnp.int32)
    following = jnp.roll(order, -1)
    cycle = jnp.zeros((PACKS * DOCS,), jnp.int32).at[order].set(following)
    return cycle.reshape(PACKS, DOCS)


def touch_ends(drawn, key, least, high):
    spot = [jax.random.randint(jax.random.fold_in(key, axis), (), 0, length) for axis, length in enumerate(drawn.shape)]
    main_axis = drawn.shape.index(max(drawn.shape))
    next_to = spot[:main_axis] + [(spot[main_axis] + 1) % drawn.shape[main_axis]] + spot[main_axis + 1:]
    return drawn.at[tuple(spot)].set(least).at[tuple(next_to)].set(high)


def steps_of(rng, dims, pieces, least, high):
    def one(axis_at, shards_of):
        draws = jax.random.uniform(jax.random.fold_in(jax.random.fold_in(rng, 6), axis_at), (shards_of,), jnp.float32, least / len(pieces), high / len(pieces))
        return jnp.repeat(jnp.exp(draws), dims[axis_at] // shards_of).reshape((-1,) + (1,) * (len(dims) - axis_at - 1))

    factor_of = one(*pieces[0])
    for cut in pieces[1:]:
        factor_of = factor_of * one(*cut)
    return factor_of


def profile(amount, total, bound, lean):
    loads = [(1 << 20) // math.isqrt(rank ** lean) + 1 for rank in range(2, amount + 1)]
    spare, holding = total - bound - (amount - 1), [1] * (amount - 1)
    while spare > 0:
        candidates = [i for i in range(amount - 1) if holding[i] < bound]
        pool, budget = sum([loads[i] for i in candidates]), spare
        for i in candidates:
            more = min(bound - holding[i], max(1, budget * loads[i] // pool), spare)
            holding[i] = holding[i] + more
            spare = spare - more
    return np.array([bound] + holding)


def ragged(stream_key, amount, total, limit, slope):
    if amount == 2:
        one = jax.random.randint(stream_key, (), max(1, total - limit), min(limit, total - 1) + 1)
        return jnp.stack([one, total - one])
    sizes = jnp.asarray(profile(amount, total, limit, slope), jnp.int32)
    pairs = (amount - 1) // 2
    donor, receiver = sizes[1:1 + 2 * pairs:2], sizes[2:2 + 2 * pairs:2]
    slack = jnp.minimum(donor - 1, limit - receiver)
    passed = jax.random.randint(jax.random.fold_in(stream_key, 1), (pairs,), 0, 1 << 20) % (slack + 1)
    sizes = sizes.at[1:1 + 2 * pairs:2].set(donor - passed).at[2:2 + 2 * pairs:2].set(receiver + passed)
    return sizes[jax.random.permutation(jax.random.fold_in(stream_key, 2), amount)]


def centred(stream_key, shape, scale, limit, pieces=(), kind=jnp.bfloat16):
    array = jax.random.normal(stream_key, shape, jnp.float32) * scale
    if len(pieces) > 0:
        array = steps_of(stream_key, shape, pieces, -0.22, 0.18) * array
    return jnp.clip(array, min=-limit, max=limit).astype(kind)


def setup_inputs(seed: int = 0) -> dict:
    key_list = jax.random.split(jax.random.key(seed), 8)
    return {
        "queries": draw_queries(jax.random.fold_in(key_list[7], 71), 0),
        "keys": draw_keys(jax.random.fold_in(key_list[7], 71), 0),
        "values": centred(key_list[2], (PACKS, LEN, KVD), 1.0, 5.0, ((0, 32), (1, 8))),
        "out_grad": centred(key_list[3], (PACKS, LEN, DQ), 0.02, 0.119628906, ((0, 32), (1, 8))),
        "doc_blocks": jax.vmap(lambda own: ragged(own, DOCS, LEN // BLOCK, LEN // BLOCK // 2, 2))(jax.random.split(key_list[4], PACKS)).reshape((PACKS, DOCS)).astype(jnp.int32),
        "pad_count": touch_ends(jax.random.randint(key_list[5], (PACKS, DOCS), 0, BLOCK), jax.random.fold_in(key_list[5], 1), 0, BLOCK - 1).astype(jnp.int32),
        "partner": draw_partner(jax.random.fold_in(key_list[7], 71), 0),
    }


temper = 0.05
eps_mean = 1e-06

def pack_ids(blocks):
    ends = (jnp.cumsum(blocks) * BLOCK).astype(jnp.int32)
    position = jnp.arange(LEN, dtype=jnp.int32)
    ids = lax.optimization_barrier(jnp.sum((position[:, None] >= ends[None, :]).astype(jnp.int32), axis=1)).astype(jnp.int32)
    return (ends, ids)

def head_probs(q_four, k_three, ids):
    scores = jnp.einsum('qngd,knd->ngqk', q_four.astype(jnp.float32), k_three.astype(jnp.float32)) * HD ** (-0.5)
    same = ids[:, None] == ids[None, :]
    peak = lax.optimization_barrier(jnp.max(jnp.where(same, scores, -jnp.inf), axis=-1, keepdims=True))
    weights = jnp.where(same, jnp.exp(scores - peak), 0.0)
    return weights / lax.optimization_barrier(jnp.sum(weights, axis=-1, keepdims=True))

def forward_pack(operands):
    query, key_rows, value_rows, blocks = operands
    ends, ids = pack_ids(blocks)
    q_four = query.reshape(LEN, KVH, HQ // KVH, HD)
    k_three = key_rows.reshape(LEN, KVH, HD)
    v_three = value_rows.reshape(LEN, KVH, HD)
    probs = head_probs(q_four, k_three, ids).astype(jnp.bfloat16)
    out = jnp.einsum('ngqk,knd->qngd', probs.astype(jnp.float32), v_three.astype(jnp.float32))
    return out.astype(jnp.bfloat16).reshape(LEN, DQ)

def contrast(dots, own_scale, scale_all, partner_row, base):
    sim = dots * own_scale[:, None] * scale_all[None, :] / (DQ * temper)
    column = jnp.arange(scale_all.shape[0], dtype=jnp.int32)[None, :]
    own_index = base + jnp.arange(dots.shape[0], dtype=jnp.int32)
    weights = jnp.where(column == own_index[:, None], 0.0, jnp.exp(sim - 1.0 / temper))
    total = lax.optimization_barrier(jnp.sum(weights, axis=1))
    chosen = jnp.where(column == partner_row[:, None], 1.0, 0.0)
    return weights / total[:, None] - chosen

def embed_grad(emb, mixed, scale, inner):
    return (scale / (DQ * temper))[:, None] * (mixed - (scale * scale * inner / DQ)[:, None] * emb)

def backward_pack(operands):
    query, key_rows, value_rows, grad_rows, blocks, attn, pooled_pos, grad = operands
    ends, ids = pack_ids(blocks)
    total = grad_rows.astype(jnp.float32).at[pooled_pos].add(grad).astype(jnp.bfloat16)
    q_four = query.reshape(LEN, KVH, HQ // KVH, HD)
    k_three = key_rows.reshape(LEN, KVH, HD)
    v_three = value_rows.reshape(LEN, KVH, HD)
    g_four = total.reshape(LEN, KVH, HQ // KVH, HD)
    o_four = attn.reshape(LEN, KVH, HQ // KVH, HD)
    probs = head_probs(q_four, k_three, ids)
    probs_low = probs.astype(jnp.bfloat16)
    delta = lax.optimization_barrier(jnp.sum(g_four.astype(jnp.float32) * o_four.astype(jnp.float32), axis=-1))
    dprob = jnp.einsum('qngd,knd->ngqk', g_four.astype(jnp.float32), v_three.astype(jnp.float32))
    dscore = (probs * (dprob - jnp.transpose(delta, (1, 2, 0))[..., None])).astype(jnp.bfloat16)
    dq = jnp.einsum('ngqk,knd->qngd', dscore.astype(jnp.float32), k_three.astype(jnp.float32)) * HD ** (-0.5)
    dk = jnp.einsum('ngqk,qngd->knd', dscore.astype(jnp.float32), q_four.astype(jnp.float32)) * HD ** (-0.5)
    dv = jnp.einsum('ngqk,qngd->knd', probs_low.astype(jnp.float32), g_four.astype(jnp.float32))
    return (dq.astype(jnp.bfloat16).reshape(LEN, DQ), dk.astype(jnp.bfloat16).reshape(LEN, KVD), dv.astype(jnp.bfloat16).reshape(LEN, KVD))

def reference(queries, keys, values, out_grad, doc_blocks, pad_count, partner):
    attn = lax.map(forward_pack, (queries, keys, values, doc_blocks))
    ends = (jnp.cumsum(doc_blocks, axis=1) * BLOCK).astype(jnp.int32)
    pooled_pos = (ends - 1 - pad_count).astype(jnp.int32)
    emb = jax.vmap(lambda rows, where_at: rows[where_at])(attn, pooled_pos)
    emb = emb.astype(jnp.float32).reshape(POOLED, DQ)
    scale = lax.rsqrt(lax.optimization_barrier(jnp.mean(emb * emb, axis=1)) + eps_mean)
    dots = jnp.dot(emb, emb.T, precision=lax.Precision.HIGHEST)
    attract = contrast(dots, scale, scale, partner.reshape(POOLED), 0)
    scaled = scale[:, None] * emb
    mixed = jnp.dot(attract, scaled, precision=lax.Precision.HIGHEST) + jnp.dot(attract.T, scaled, precision=lax.Precision.HIGHEST)
    inner = lax.optimization_barrier(jnp.sum(emb * mixed, axis=1))
    grad = embed_grad(emb, mixed, scale, inner).reshape(PACKS, DOCS, DQ)
    dq, dk, dv = lax.map(backward_pack, (queries, keys, values, out_grad, doc_blocks, attn, pooled_pos, grad))
    return (dq, dk, dv)
```

```python
import functools
import math

import jax
import jax.numpy as jnp
from jax import lax
from jax.experimental import pallas as pl
from jax.experimental.pallas import tpu as pltpu
from jax.sharding import PartitionSpec as P

HQ = 32
KVH = 8
HD = 128
BLOCK = 128
DQ = 4096
SEQ = 8
GROUP = HQ // KVH
WIDTH = GROUP * HD
LEN = SEQ * BLOCK
WINDOW = 4
temper = 0.05
eps_mean = 1e-06

NEG = -1e30
LOG2E = math.log2(math.e)
SCALE = HD ** (-0.5)
bf16 = jnp.bfloat16
f32 = jnp.float32
i32 = jnp.int32
HIGHEST = lax.Precision.HIGHEST

SMEM = pl.BlockSpec(memory_space=pltpu.SMEM)
VMEM = pl.BlockSpec(memory_space=pltpu.VMEM)


def call(body, out, n_smem, n_in, flops=0, moved=0, scratch=()):
    single = not isinstance(out, (list, tuple))
    return pl.pallas_call(
        body,
        out_shape=out,
        in_specs=[SMEM] * n_smem + [VMEM] * n_in,
        out_specs=VMEM if single else [VMEM] * len(out),
        scratch_shapes=list(scratch),
        compiler_params=pltpu.CompilerParams(vmem_limit_bytes=40 * 2**20),
        cost_estimate=pl.CostEstimate(flops=flops, bytes_accessed=moved, transcendentals=0),
    )


def shape(*dims, dtype=bf16):
    return jax.ShapeDtypeStruct(dims, dtype)


def iota(dims, axis):
    return lax.broadcasted_iota(i32, dims, axis)


def dot(a, b, dims, precision=None):
    return lax.dot_general(a, b, ((dims[:1], dims[1:]), ((), ())), precision=precision, preferred_element_type=f32)


def doc_ends(blocks):
    first = blocks[0, 0]
    second = first + blocks[0, 1]
    return first, second, second + blocks[0, 2]


def pooled_rows(blocks, pad):
    return [end * BLOCK - 1 - pad[0, doc] for doc, end in enumerate(doc_ends(blocks))]


def fold(rows):
    left = jnp.concatenate([rows[:, 0:128], rows[:, 128:256]], axis=0)
    right = jnp.concatenate([rows[:, 256:384], rows[:, 384:512]], axis=0)
    return jnp.concatenate([left, right], axis=1)


def by_head(folded):
    return jnp.concatenate([folded[:, 0:128], folded[:, 128:256]], axis=0)


def pack_first(me, blocks, pad, q, k, v, g, out):
    here = me[0] * BLOCK
    row, col = iota((8, BLOCK), 0), iota((8, BLOCK), 1)
    hot = jnp.zeros((8, BLOCK), f32)
    for doc, at in enumerate(pooled_rows(blocks, pad)):
        hot = jnp.where((row == doc) & (col == at - here), 1.0, hot)
    hot = hot.astype(bf16)
    q_rows = dot(hot, q[...], (1, 0))
    g_rows = dot(hot, g[...], (1, 0))
    for s in range(SEQ):
        out[s, 0:128, 0:128] = k[:, s * HD:(s + 1) * HD]
        out[s, 0:128, 128:256] = v[:, s * HD:(s + 1) * HD]
        out[s, 128:144, :] = fold(q_rows[:, s * WIDTH:(s + 1) * WIDTH]).astype(bf16)
        out[s, 144:160, :] = fold(g_rows[:, s * WIDTH:(s + 1) * WIDTH]).astype(bf16)


def pack_rest(me, q, g, *outs):
    for k in range(SEQ):
        at = pl.ds(pl.multiple_of((me[0] ^ k) * WIDTH, WIDTH), WIDTH)
        outs[k][:, 0:WIDTH] = q[:, at]
        outs[k][:, WIDTH:2 * WIDTH] = g[:, at]


def pooled_forward(blocks, partner, recv, emb, probs, q_rows, g_rows):
    q_sum = jnp.zeros((16, 256), f32)
    g_sum = jnp.zeros((16, 256), f32)
    for s in range(SEQ):
        q_sum = q_sum + recv[s, 128:144, :].astype(f32)
        g_sum = g_sum + recv[s, 144:160, :].astype(f32)
    q_low = by_head(q_sum).astype(bf16)
    q_rows[...] = q_low
    g_rows[...] = by_head(g_sum).astype(bf16)
    keys = jnp.concatenate([recv[s, 0:128, 0:128] for s in range(SEQ)], axis=0)
    vals = jnp.concatenate([recv[s, 0:128, 128:256] for s in range(SEQ)], axis=0)
    first, second, last = doc_ends(blocks)
    doc = iota((32, LEN), 0) & 7
    block = iota((32, LEN), 1) >> 7
    low = jnp.where(doc == 0, 0, jnp.where(doc == 1, first, second))
    high = jnp.where(doc == 0, first, jnp.where(doc == 1, second, last))
    scores = dot(q_low, keys, (1, 1)) * (SCALE * LOG2E)
    scores = jnp.where((block >= low) & (block < high), scores, NEG)
    peak = jnp.max(scores, axis=1, keepdims=True)
    weights = jnp.exp2(scores - peak)
    p = weights / jnp.sum(weights, axis=1, keepdims=True)
    probs[...] = p
    out = dot(p.astype(bf16), vals, (1, 0)).astype(bf16)
    row, col = iota((16, 32), 0), iota((16, 32), 1)
    pick = jnp.where((col == (row >> 2) * 8 + (row & 3)) & ((row & 3) < 3), 1.0, 0.0).astype(bf16)
    rows = dot(pick, out, (1, 0))
    row, lane = iota((16, HD), 0), iota((16, HD), 1)
    for d in range(3):
        index = partner[0, d]
        spot = (lax.div(index, 3) * 4 + lax.rem(index, 3)).astype(f32)
        rows = jnp.where((row == 3) & (lane == d), spot, rows)
    rows = rows.astype(bf16)
    for copy in range(emb.shape[0]):
        emb[copy] = rows


def gram_part(rows, heads, part):
    packs = rows.shape[0]
    n = packs * 4
    flat = rows[...].reshape(packs * 16, HD)
    r, c = iota((4 * n, packs * 16), 0), iota((4 * n, packs * 16), 1)
    i, h = r & (n - 1), r // n
    hit = (c == (i >> 2) * 16 + h * 4 + (i & 3)) & ((i & 3) < 3)
    mixed = dot(jnp.where(hit, 1.0, 0.0).astype(bf16), flat, (1, 0)).astype(bf16)
    heads[...] = mixed
    total = jnp.zeros((n, n), f32)
    for h in range(GROUP):
        e = mixed[h * n:(h + 1) * n]
        total = total + dot(e, e, (1, 1))
    for s in range(SEQ):
        part[s] = total


def main_kernel(me, blocks, pad, recv, *refs):
    rows, (dk, dv), dqs = refs[:SEQ], refs[SEQ:SEQ + 2], refs[SEQ + 2:]
    first, second, last = doc_ends(blocks)
    spots = pooled_rows(blocks, pad)
    dk[...] = jnp.zeros_like(dk)
    dv[...] = jnp.zeros_like(dv)
    for k in range(SEQ):
        b = me[0] ^ k
        low = jnp.where(b < first, 0, jnp.where(b < second, first, second))
        high = jnp.where(b < first, first, jnp.where(b < second, second, last))
        start = jnp.minimum(low, SEQ - WINDOW)
        keys = jnp.concatenate([recv[start + j, 0:128, 0:128] for j in range(WINDOW)], axis=0)
        vals = jnp.concatenate([recv[start + j, 0:128, 128:256] for j in range(WINDOW)], axis=0)
        q = jnp.concatenate([rows[k][:, h * HD:(h + 1) * HD] for h in range(GROUP)], axis=0)
        g = jnp.concatenate([rows[k][:, WIDTH + h * HD:WIDTH + (h + 1) * HD] for h in range(GROUP)], axis=0)
        at = iota((GROUP * BLOCK, HD), 0) & (BLOCK - 1)
        pooled = (at == spots[0] - b * BLOCK) | (at == spots[1] - b * BLOCK) | (at == spots[2] - b * BLOCK)
        g = jnp.where(pooled, 0.0, g.astype(f32)).astype(bf16)
        scores = dot(keys, q, (1, 1)) * (SCALE * LOG2E)
        parts = []
        for j in range(WINDOW):
            seen = (start + j >= low) & (start + j < high)
            parts.append(scores[j * BLOCK:(j + 1) * BLOCK] + jnp.where(seen, 0.0, NEG))
        scores = jnp.concatenate(parts, axis=0)
        peak = jnp.max(scores, axis=0, keepdims=True)
        weights = jnp.exp2(scores - peak)
        probs = weights * (1.0 / jnp.sum(weights, axis=0, keepdims=True))
        dprob = dot(vals, g, (1, 1))
        delta = jnp.sum(probs * dprob, axis=0, keepdims=True)
        dscore = (probs * (dprob - delta)).astype(bf16)
        dq = dot(dscore, keys, (0, 0)) * SCALE
        for h in range(GROUP):
            dqs[k][:, h * HD:(h + 1) * HD] = dq[h * BLOCK:(h + 1) * BLOCK].astype(bf16)
        dk_add = dot(dscore, q, (1, 0))
        dv_add = dot(probs.astype(bf16), g, (1, 0))
        for j in range(WINDOW):
            dk[start + j] += dk_add[j * BLOCK:(j + 1) * BLOCK]
            dv[start + j] += dv_add[j * BLOCK:(j + 1) * BLOCK]


def finish(pack, raw, heads, parts, probs_ref, q_rows, g_rows, recv, dk, dv, out):
    packs = raw.shape[0]
    n = packs * 4
    gram = parts[0]
    for s in range(1, SEQ):
        gram = gram + parts[s]
    row, col = iota((n, n), 0), iota((n, n), 1)
    flat = raw[...].reshape(packs * 16, HD)
    r, c = iota((n, packs * 16), 0), iota((n, packs * 16), 1)
    hit = jnp.where(c == (r >> 2) * 16 + 3, 1.0, 0.0).astype(bf16)
    spots = dot(hit, flat, (1, 0))
    r, c = iota((n, HD), 0), iota((n, HD), 1)
    partner = jnp.sum(jnp.where(c == (r & 3), spots, 0.0), axis=1, keepdims=True)
    real_row, real_col = (row & 3) < 3, (col & 3) < 3
    chosen = jnp.where((partner.astype(i32) == col) & real_row, 1.0, 0.0)
    squares = jnp.where(row == col, gram, 0.0)
    square_row = jnp.sum(squares, axis=1, keepdims=True)
    square_col = jnp.sum(squares, axis=0, keepdims=True)
    scale_row = lax.rsqrt(square_row / DQ + eps_mean)
    scale_col = lax.rsqrt(square_col / DQ + eps_mean)
    sim = gram * scale_row * scale_col / (DQ * temper)
    weight = jnp.where((row != col) & real_row & real_col, jnp.exp(sim - 1.0 / temper), 0.0)
    total = jnp.sum(weight, axis=1, keepdims=True)
    attract = weight / jnp.where((iota((n, 1), 0) & 3) < 3, total, 1.0) - chosen
    terms = (attract + attract.T) * scale_col
    inner = jnp.sum(terms * gram, axis=1, keepdims=True)
    own = jnp.where(row == col, scale_row * scale_row * inner / DQ, 0.0)
    mix = scale_row / (DQ * temper) * (terms - own)
    r, c = iota((8, n), 0), iota((8, n), 1)
    pick = jnp.where((c == pack[0] * 4 + r) & (r < 3), 1.0, 0.0)
    mix = dot(pick, mix, (1, 0), HIGHEST)
    grads = [dot(mix, heads[h * n:(h + 1) * n].astype(f32), (1, 0), HIGHEST) for h in range(GROUP)]
    g = (g_rows[...].astype(f32) + jnp.concatenate(grads, axis=0)).astype(bf16)

    keys = jnp.concatenate([recv[s, 0:128, 0:128] for s in range(SEQ)], axis=0)
    vals = jnp.concatenate([recv[s, 0:128, 128:256] for s in range(SEQ)], axis=0)
    probs = probs_ref[...]
    dprob = dot(g, vals, (1, 1))
    delta = jnp.sum(probs * dprob, axis=1, keepdims=True)
    dscore = (probs * (dprob - delta)).astype(bf16)
    dq = dot(dscore, keys, (1, 0)) * SCALE
    dk_add = dot(dscore, q_rows[...], (0, 0))
    dv_add = dot(probs.astype(bf16), g, (0, 0))
    left = jnp.concatenate([dq[0:8], dq[8:16]], axis=0)
    right = jnp.concatenate([dq[16:24], dq[24:32]], axis=0)
    dq = jnp.concatenate([left, right], axis=1).astype(bf16)
    for s in range(SEQ):
        at = slice(s * BLOCK, (s + 1) * BLOCK)
        out[s, 0:128, 0:128] = ((dk[s] + dk_add[at]) * SCALE).astype(bf16)
        out[s, 0:128, 128:256] = (dv[s] + dv_add[at]).astype(bf16)
        out[s, 128:144, :] = dq


def unpack(me, blocks, pad, recv, *refs):
    rows, (dq, dk, dv) = refs[:SEQ], refs[SEQ:]
    here = me[0] * BLOCK
    row, col = iota((BLOCK, 8), 0), iota((BLOCK, 8), 1)
    hot = jnp.zeros((BLOCK, 8), f32)
    for doc, at in enumerate(pooled_rows(blocks, pad)):
        hot = jnp.where((col == doc) & (row == at - here), 1.0, hot)
    hot = hot.astype(bf16)
    for k in range(SEQ):
        s = me[0] ^ k
        fixed = by_head(recv[s, 128:144, :].astype(f32))
        fixed = jnp.concatenate([fixed[8 * h:8 * h + 8] for h in range(GROUP)], axis=1).astype(bf16)
        patched = rows[k][...].astype(f32) + dot(hot, fixed, (1, 0))
        dq[:, pl.ds(pl.multiple_of(s * WIDTH, WIDTH), WIDTH)] = patched.astype(bf16)
    for s in range(SEQ):
        dk[:, s * HD:(s + 1) * HD] = recv[s, 0:128, 0:128]
        dv[:, s * HD:(s + 1) * HD] = recv[s, 0:128, 128:256]


def exchange(x, axis, **kw):
    return lax.all_to_all(x, axis, split_axis=0, concat_axis=0, tiled=True, **kw)


def swap(x, k):
    return lax.ppermute(x, "seq", [(s, s ^ k) for s in range(SEQ)])


FAR_FIRST = (1, 2, 3, 6, 7, 4, 5)


def on_device(n_dp, queries, keys, values, out_grad, doc_blocks, pad_count, partner):
    me = lax.axis_index("seq").astype(i32).reshape(1)
    pack = lax.axis_index("dp").astype(i32).reshape(1)
    q, k, v, g = queries[0], keys[0], values[0], out_grad[0]
    send = call(pack_first, shape(SEQ, 160, 256), 3, 4)(me, doc_blocks, pad_count, q, k, v, g)
    recv = exchange(send, "seq")
    mine = call(pack_rest, [shape(BLOCK, 2 * WIDTH)] * SEQ, 1, 2, moved=2 * 2**20)(me, q, g)
    rows = [mine[0]] + [None] * (SEQ - 1)
    for step in FAR_FIRST:
        rows[step] = swap(mine[step], step)

    near = 4 if n_dp % 4 == 0 else n_dp
    far = n_dp // near
    emb, probs, q_rows, g_rows = call(
        pooled_forward,
        [shape(near, 16, HD), shape(32, LEN, dtype=f32), shape(32, HD), shape(32, HD)],
        2, 1, moved=2**20,
    )(doc_blocks, partner, recv)
    inner_groups = [[far_at * near + i for i in range(near)] for far_at in range(far)]
    emb = exchange(emb, "dp", axis_index_groups=inner_groups)
    if far > 1:
        outer_groups = [[far_at * near + i for far_at in range(far)] for i in range(near)]
        emb = jnp.broadcast_to(emb.reshape(1, near * 16, HD), (far, near * 16, HD))
        emb = exchange(emb, "dp", axis_index_groups=outer_groups)
    emb = emb.reshape(n_dp, 16, HD)
    n = 4 * n_dp
    heads, part = call(gram_part, [shape(GROUP * n, HD), shape(SEQ, n, n, dtype=f32)], 0, 1, moved=2**20)(emb)
    parts = exchange(part, "seq")

    dk, dv, *dqs = call(
        main_kernel,
        [shape(SEQ, BLOCK, HD, dtype=f32)] * 2 + [shape(BLOCK, WIDTH)] * SEQ,
        3, SEQ + 1, flops=5 * 2**32, moved=8 * 2**20,
    )(me, doc_blocks, pad_count, recv, *rows)
    back = [dqs[0]] + [None] * (SEQ - 1)
    for step in FAR_FIRST:
        back[step] = swap(dqs[step], step)
    send = call(finish, shape(SEQ, 144, 256), 1, 9, moved=2**21)(
        pack, emb, heads, parts, probs, q_rows, g_rows, recv, dk, dv
    )
    recv = exchange(send, "seq")
    dq, dk, dv = call(
        unpack, [shape(BLOCK, DQ), shape(BLOCK, KVH * HD), shape(BLOCK, KVH * HD)], 3, SEQ + 1, moved=4 * 2**20
    )(me, doc_blocks, pad_count, recv, *back)
    return dq[None], dk[None], dv[None]


def solution(mesh):
    rows = P("dp", "seq", None)
    return jax.shard_map(
        functools.partial(on_device, mesh.shape["dp"]),
        mesh=mesh,
        in_specs=(rows, rows, rows, rows, P("dp", None), P("dp", None), P("dp", None)),
        out_specs=(rows, rows, rows),
        check_vma=False,
    )
```

```python
import functools
import math

import jax
import jax.numpy as jnp
from jax import lax
from jax.experimental import pallas as pl
from jax.experimental.pallas import tpu as pltpu
from jax.sharding import PartitionSpec as P

HQ = 32
KVH = 8
HD = 128
BLOCK = 128
DQ = 4096
SEQ = 8
GROUP = HQ // KVH
WIDTH = GROUP * HD
LEN = SEQ * BLOCK
WINDOW = 4
temper = 0.05
eps_mean = 1e-06

ORDER = (1, 4, 5, 2, 3, 6, 7)
NEG = -1e30
LOG2E = math.log2(math.e)
SCALE = HD ** (-0.5)
bf16 = jnp.bfloat16
f32 = jnp.float32
i32 = jnp.int32
HIGHEST = lax.Precision.HIGHEST
LARGE = 60 * 2**20
SMALL = 24 * 2**20

SPACES = {
    "s": pl.BlockSpec(memory_space=pltpu.SMEM),
    "v": pl.BlockSpec(memory_space=pltpu.VMEM),
    "a": pl.BlockSpec(memory_space=pl.ANY),
}


def call(body, ins, out, outs, args, scratch=(), flops=0, limit=SMALL):
    single = not isinstance(out, (list, tuple))
    places = [SPACES[c] for c in outs]
    return pl.pallas_call(
        body,
        out_shape=out,
        in_specs=[SPACES[c] for c in ins],
        out_specs=places[0] if single else places,
        scratch_shapes=list(scratch),
        compiler_params=pltpu.CompilerParams(vmem_limit_bytes=limit),
        cost_estimate=pl.CostEstimate(flops=flops, bytes_accessed=2**20, transcendentals=0),
    )(*args)


def shape(*dims, dtype=bf16):
    return jax.ShapeDtypeStruct(dims, dtype)


def iota(dims, axis):
    return lax.broadcasted_iota(i32, dims, axis)


def dot(a, b, dims, precision=None):
    return lax.dot_general(a, b, ((dims[:1], dims[1:]), ((), ())), precision=precision, preferred_element_type=f32)


def doc_ends(blocks):
    first = blocks[0, 0]
    second = first + blocks[0, 1]
    return first, second, second + blocks[0, 2]


def choose(b, ends, at_first, at_second, at_last):
    return jnp.where(b < ends[0], at_first, jnp.where(b < ends[1], at_second, at_last))


def own_pooled(b, blocks, pad):
    ends = doc_ends(blocks)
    doc = choose(b, ends, 0, 1, 2)
    at = choose(b, ends, *(end * BLOCK - 1 - pad[0, d] for d, end in enumerate(ends))) - b * BLOCK
    here = (at >= 0) & (at < BLOCK)
    return doc, jnp.clip(at, 0, BLOCK - 1), here


def pack_first(me, blocks, pad, k, v, q, g, out, near, q_slab, g_slab, sems, in_sems, out_sem):
    doc, at, here = own_pooled(me[0], blocks, pad)
    base = pl.multiple_of((at >> 4) * 16, 16)
    slabs = (q_slab, g_slab)
    fetch = [pltpu.make_async_copy(far.at[pl.ds(base, 16), :], slabs[i], sems.at[i]) for i, far in enumerate((q, g))]
    for s in range(SEQ):
        for i, far in enumerate((k, v)):
            fetch.append(pltpu.make_async_copy(
                far.at[:, pl.ds(s * HD, HD)], near.at[s, pl.ds(0, BLOCK), pl.ds(i * HD, HD)], in_sems.at[2 * s + i]
            ))
    for copy in fetch:
        copy.start()
    hot = jnp.where((iota((8, 16), 1) == at - base) & here, 1.0, 0.0).astype(bf16)
    row = iota((16, HD), 0)
    for i in range(2):
        fetch[i].wait()
        line = dot(hot, slabs[i][...], (1, 0))[0:1]
        for s in range(SEQ):
            rows = jnp.zeros((16, HD), f32)
            for h in range(GROUP):
                piece = line[:, s * WIDTH + h * HD:s * WIDTH + (h + 1) * HD]
                rows = jnp.where(row == h * 4 + doc, piece, rows)
            near[s, 128:144, i * HD:(i + 1) * HD] = rows.astype(bf16)
    for copy in fetch[2:]:
        copy.wait()
    back = pltpu.make_async_copy(near, out, out_sem.at[0])
    back.start()
    back.wait()


def pack_rest(me, q, g, _, *refs):
    outs, stage, in_sems, out_sems = refs[:SEQ], refs[SEQ], refs[SEQ + 1], refs[SEQ + 2]
    arriving, leaving = [], []
    for k in (*ORDER, 0):
        at = pl.ds(pl.multiple_of((me[0] ^ k) * WIDTH, WIDTH), WIDTH)
        arriving.append((
            pltpu.make_async_copy(q.at[:, at], stage.at[k, :, pl.ds(0, WIDTH)], in_sems.at[2 * k]),
            pltpu.make_async_copy(g.at[:, at], stage.at[k, :, pl.ds(WIDTH, WIDTH)], in_sems.at[2 * k + 1]),
        ))
        leaving.append(pltpu.make_async_copy(stage.at[k], outs[k], out_sems.at[k]))
    for pair in arriving:
        for copy in pair:
            copy.start()
    for pair, copy in zip(arriving, leaving):
        for one in pair:
            one.wait()
        copy.start()
    for copy in leaving:
        copy.wait()


def pooled_forward(blocks, partner, recv, _, emb, probs, q_rows, g_rows):
    both = jnp.zeros((16, 2 * HD), f32)
    for s in range(SEQ):
        both = both + recv[s, 128:144, :].astype(f32)
    q_low = both[:, 0:HD].astype(bf16)
    q_rows[...] = q_low
    g_rows[...] = both[:, HD:2 * HD].astype(bf16)
    keys = jnp.concatenate([recv[s, 0:128, 0:128] for s in range(SEQ)], axis=0)
    vals = jnp.concatenate([recv[s, 0:128, 128:256] for s in range(SEQ)], axis=0)
    first, second, last = doc_ends(blocks)
    doc = iota((16, LEN), 0) & 3
    block = iota((16, LEN), 1) >> 7
    low = jnp.where(doc == 0, 0, jnp.where(doc == 1, first, second))
    high = jnp.where(doc == 0, first, jnp.where(doc == 1, second, last))
    scores = dot(q_low, keys, (1, 1)) * (SCALE * LOG2E)
    scores = jnp.where((block >= low) & (block < high), scores, NEG)
    peak = jnp.max(scores, axis=1, keepdims=True)
    weights = jnp.exp2(scores - peak)
    p = weights / jnp.sum(weights, axis=1, keepdims=True)
    probs[...] = p
    rows = dot(p.astype(bf16), vals, (1, 0)).astype(bf16).astype(f32)
    row, lane = iota((16, HD), 0), iota((16, HD), 1)
    rows = jnp.where((row & 3) < 3, rows, 0.0)
    for d in range(3):
        index = partner[0, d]
        spot = (lax.div(index, 3) * 4 + lax.rem(index, 3)).astype(f32)
        rows = jnp.where((row == 3) & (lane == d), spot, rows)
    rows = rows.astype(bf16)
    for copy in range(emb.shape[0]):
        emb[copy] = rows


def gram_part(rows, _, heads, part):
    packs = rows.shape[0]
    n = packs * 4
    flat = rows[...].reshape(packs * 16, HD)
    r, c = iota((4 * n, packs * 16), 0), iota((4 * n, packs * 16), 1)
    i, h = r & (n - 1), r // n
    hit = (c == (i >> 2) * 16 + h * 4 + (i & 3)) & ((i & 3) < 3)
    mixed = dot(jnp.where(hit, 1.0, 0.0).astype(bf16), flat, (1, 0)).astype(bf16)
    heads[...] = mixed
    total = jnp.zeros((n, n), f32)
    for h in range(GROUP):
        e = mixed[h * n:(h + 1) * n]
        total = total + dot(e, e, (1, 1))
    half = n // 2
    row, col = iota((n, n), 0), iota((n, n), 1)
    diagonal = jnp.sum(jnp.where(row == col, total, 0.0), axis=0, keepdims=True)
    row, col = iota((half, n), 0), iota((half, n), 1)
    turned = pltpu.roll(total[half:], half, 1)
    packed = jnp.where(row >= col, total[:half], turned)
    packed = jnp.where(col >= half, jnp.where(row == 3, diagonal, total[:half]), packed)
    for s in range(SEQ):
        part[s] = packed


def unpack_gram(packed):
    half, n = packed.shape
    row, col = iota((n, n), 0), iota((n, n), 1)
    tall = jnp.concatenate([packed, packed], axis=0)
    turned = pltpu.roll(tall, half, 1)
    upper = (row < half) & (((col < half) & (row > col)) | ((col >= half) & (row != 3)))
    lower = (row >= half) & (row < col)
    one = jnp.where(upper, tall, 0.0) + jnp.where(lower, turned, 0.0)
    diagonal = jnp.where(row < half, tall, packed[3:4])
    return one + one.T + jnp.where(row == col, diagonal, 0.0)


def attend(me, blocks, pad, steps, recv, rows, dk, dv, outs):
    ends = doc_ends(blocks)
    for k, row, out in zip(steps, rows, outs):
        b = me[0] ^ k
        low = choose(b, ends, 0, ends[0], ends[1])
        high = choose(b, ends, *ends)
        _, spot, here = own_pooled(b, blocks, pad)
        start = jnp.minimum(low, SEQ - WINDOW)
        keys = jnp.concatenate([recv[start + j, 0:128, 0:128] for j in range(WINDOW)], axis=0)
        vals = jnp.concatenate([recv[start + j, 0:128, 128:256] for j in range(WINDOW)], axis=0)
        q = jnp.concatenate([row[:, h * HD:(h + 1) * HD] for h in range(GROUP)], axis=0)
        g = jnp.concatenate([row[:, WIDTH + h * HD:WIDTH + (h + 1) * HD] for h in range(GROUP)], axis=0)
        pooled = ((iota((GROUP * BLOCK, HD), 0) & (BLOCK - 1)) == spot) & here
        g = jnp.where(pooled, 0.0, g.astype(f32)).astype(bf16)
        dscores, probs_low = [], []
        for at in range(0, WIDTH, 2 * HD):
            scores = dot(keys, q[at:at + 2 * HD], (1, 1)) * (SCALE * LOG2E)
            parts = []
            for j in range(WINDOW):
                seen = (start + j >= low) & (start + j < high)
                parts.append(scores[j * BLOCK:(j + 1) * BLOCK] + jnp.where(seen, 0.0, NEG))
            scores = jnp.concatenate(parts, axis=0)
            peak = jnp.max(scores, axis=0, keepdims=True)
            weights = jnp.exp2(scores - peak)
            probs = weights * (1.0 / jnp.sum(weights, axis=0, keepdims=True))
            dprob = dot(vals, g[at:at + 2 * HD], (1, 1))
            delta = jnp.sum(probs * dprob, axis=0, keepdims=True)
            dscores.append((probs * (dprob - delta)).astype(bf16))
            probs_low.append(probs.astype(bf16))
        dscore = jnp.concatenate(dscores, axis=1)
        dq = dot(dscore, keys, (0, 0)) * SCALE
        for h in range(GROUP):
            out[:, h * HD:(h + 1) * HD] = dq[h * BLOCK:(h + 1) * BLOCK].astype(bf16)
        dk_add = dot(dscore, q, (1, 0))
        dv_add = dot(jnp.concatenate(probs_low, axis=1), g, (1, 0))
        for j in range(WINDOW):
            dk[start + j] += dk_add[j * BLOCK:(j + 1) * BLOCK]
            dv[start + j] += dv_add[j * BLOCK:(j + 1) * BLOCK]


EARLY = (0, 1, 4, 5)
LATE = (2, 3, 6, 7)


def main_kernel(steps, first, me, blocks, pad, recv, *refs):
    n = len(steps)
    dk, dv, outs = refs[-2 - n], refs[-1 - n], refs[-n:]
    rows = refs[:n] if first else refs[2:2 + n]
    dk[...] = jnp.zeros_like(dk) if first else refs[0][...]
    dv[...] = jnp.zeros_like(dv) if first else refs[1][...]
    attend(me, blocks, pad, steps, recv, rows, dk, dv, outs)


def main_call(steps, where, recv, rows, sums, after):
    n = len(steps)
    total = shape(SEQ, BLOCK, HD, dtype=f32)
    return call(
        functools.partial(main_kernel, steps, not sums),
        "sssv" + "v" * (len(sums) + n) + "a" * len(after),
        [total, total] + [shape(BLOCK, WIDTH)] * n, "vv" + "v" * n,
        (*where, recv, *sums, *rows, *after),
        flops=6 * 10**9,
    )


def finish(pack, raw, heads, parts, probs_ref, q_rows, g_rows, recv, dk, dv, *refs):
    out = refs[-1]
    packs = raw.shape[0]
    n = packs * 4
    gram = parts[0]
    for s in range(1, SEQ):
        gram = gram + parts[s]
    gram = unpack_gram(gram)
    row, col = iota((n, n), 0), iota((n, n), 1)
    flat = raw[...].reshape(packs * 16, HD)
    r, c = iota((n, packs * 16), 0), iota((n, packs * 16), 1)
    hit = jnp.where(c == (r >> 2) * 16 + 3, 1.0, 0.0).astype(bf16)
    spots = dot(hit, flat, (1, 0))
    r, c = iota((n, HD), 0), iota((n, HD), 1)
    partner = jnp.sum(jnp.where(c == (r & 3), spots, 0.0), axis=1, keepdims=True)
    real_row, real_col = (row & 3) < 3, (col & 3) < 3
    chosen = jnp.where((partner.astype(i32) == col) & real_row, 1.0, 0.0)
    squares = jnp.where(row == col, gram, 0.0)
    square_row = jnp.sum(squares, axis=1, keepdims=True)
    square_col = jnp.sum(squares, axis=0, keepdims=True)
    scale_row = lax.rsqrt(square_row / DQ + eps_mean)
    scale_col = lax.rsqrt(square_col / DQ + eps_mean)
    sim = gram * scale_row * scale_col / (DQ * temper)
    weight = jnp.where((row != col) & real_row & real_col, jnp.exp(sim - 1.0 / temper), 0.0)
    total = jnp.sum(weight, axis=1, keepdims=True)
    attract = weight / jnp.where((iota((n, 1), 0) & 3) < 3, total, 1.0) - chosen
    terms = (attract + attract.T) * scale_col
    inner = jnp.sum(terms * gram, axis=1, keepdims=True)
    own = jnp.where(row == col, scale_row * scale_row * inner / DQ, 0.0)
    mix = scale_row / (DQ * temper) * (terms - own)
    r, c = iota((16, n), 0), iota((16, n), 1)
    pick = jnp.where((c == pack[0] * 4 + (r & 3)) & ((r & 3) < 3), 1.0, 0.0)
    mix = dot(pick, mix, (1, 0), HIGHEST)
    grad = jnp.zeros((16, HD), f32)
    r = iota((16, HD), 0)
    for h in range(GROUP):
        grad = jnp.where((r >> 2) == h, dot(mix, heads[h * n:(h + 1) * n].astype(f32), (1, 0), HIGHEST), grad)
    g = (g_rows[...].astype(f32) + grad).astype(bf16)

    keys = jnp.concatenate([recv[s, 0:128, 0:128] for s in range(SEQ)], axis=0)
    vals = jnp.concatenate([recv[s, 0:128, 128:256] for s in range(SEQ)], axis=0)
    probs = probs_ref[...]
    dprob = dot(g, vals, (1, 1))
    delta = jnp.sum(probs * dprob, axis=1, keepdims=True)
    dscore = (probs * (dprob - delta)).astype(bf16)
    dq = (dot(dscore, keys, (1, 0)) * SCALE).astype(bf16)
    dk_add = dot(dscore, q_rows[...], (0, 0))
    dv_add = dot(probs.astype(bf16), g, (0, 0))
    for s in range(SEQ):
        at = slice(s * BLOCK, (s + 1) * BLOCK)
        out[s, 0:128, 0:HD] = ((dk[s] + dk_add[at]) * SCALE).astype(bf16)
        out[s, 0:128, HD:2 * HD] = (dv[s] + dv_add[at]).astype(bf16)
        out[s, 128:144, 0:HD] = dq
        out[s, 128:144, HD:2 * HD] = dq


def assemble(me, blocks, pad, recv, *refs):
    rows, outs = refs[:SEQ], refs[SEQ:SEQ + 3]
    near, fixes, in_sems, out_sems = refs[SEQ + 3:SEQ + 6], refs[SEQ + 6], refs[SEQ + 7], refs[SEQ + 8]
    dq, dk, dv = near
    doc, at, here = own_pooled(me[0], blocks, pad)
    base = pl.multiple_of((at >> 4) * 16, 16)
    fetch = []
    for k in range(SEQ):
        s = me[0] ^ k
        lanes = pl.ds(pl.multiple_of(s * WIDTH, WIDTH), WIDTH)
        fetch.append(pltpu.make_async_copy(rows[k], dq.at[:, lanes], in_sems.at[k]))
    fetch.append(pltpu.make_async_copy(recv.at[:, pl.ds(BLOCK, 16), pl.ds(0, HD)], fixes, in_sems.at[SEQ]))
    for i, to in enumerate((dk, dv)):
        for s in range(SEQ):
            fetch.append(pltpu.make_async_copy(
                recv.at[s, pl.ds(0, BLOCK), pl.ds(i * HD, HD)], to.at[:, pl.ds(s * HD, HD)],
                in_sems.at[SEQ + 1 + i * SEQ + s],
            ))
    sends = [pltpu.make_async_copy(near[i], outs[i], out_sems.at[i]) for i in range(3)]
    for copy in fetch:
        copy.start()
    for copy in fetch[:SEQ + 1]:
        copy.wait()

    @pl.when(here)
    def _():
        row = iota((16, HD), 0)
        for s in range(SEQ):
            fixed = fixes[s].astype(f32)
            for h in range(GROUP):
                line = jnp.sum(jnp.where(row == h * 4 + doc, fixed, 0.0), axis=0, keepdims=True)
                lanes = slice(s * WIDTH + h * HD, s * WIDTH + (h + 1) * HD)
                slab = dq[pl.ds(base, 16), lanes].astype(f32)
                dq[pl.ds(base, 16), lanes] = jnp.where(row == at - base, line, slab).astype(bf16)

    sends[0].start()
    for i in (1, 2):
        for copy in fetch[SEQ + 1 + (i - 1) * SEQ:SEQ + 1 + i * SEQ]:
            copy.wait()
        sends[i].start()
    for send in sends:
        send.wait()


def exchange(x, axis, **kw):
    return lax.all_to_all(x, axis, split_axis=0, concat_axis=0, tiled=True, **kw)


def swap(x, k):
    return lax.ppermute(x, "seq", [(s, s ^ k) for s in range(SEQ)])


def on_device(n_dp, queries, keys, values, out_grad, doc_blocks, pad_count, partner):
    me = lax.axis_index("seq").astype(i32).reshape(1)
    pack = lax.axis_index("dp").astype(i32).reshape(1)
    where = (me, doc_blocks, pad_count)
    q, k, v, g = queries[0], keys[0], values[0], out_grad[0]
    pair = pltpu.SemaphoreType.DMA((2,))
    one = pltpu.SemaphoreType.DMA((1,))
    each = pltpu.SemaphoreType.DMA((SEQ,))
    double = pltpu.SemaphoreType.DMA((2 * SEQ,))
    send = call(
        pack_first, "sssaaaa", shape(SEQ, 144, 256), "a", (*where, k, v, q, g),
        scratch=[
            pltpu.VMEM((SEQ, 144, 256), bf16), pltpu.VMEM((16, DQ), bf16), pltpu.VMEM((16, DQ), bf16), pair, double, one,
        ],
        limit=LARGE,
    )
    recv = exchange(send, "seq")
    mine = call(
        pack_rest, "saaa", [shape(BLOCK, 2 * WIDTH)] * SEQ, "a" * SEQ, (me, q, g, send),
        scratch=[pltpu.VMEM((SEQ, BLOCK, 2 * WIDTH), bf16), double, each], limit=LARGE,
    )
    rows = [mine[0]] + [None] * (SEQ - 1)
    for step in ORDER:
        rows[step] = swap(mine[step], step)

    emb, probs, q_rows, g_rows = call(
        pooled_forward, "ssva",
        [shape(n_dp, 16, HD), shape(16, LEN, dtype=f32), shape(16, HD), shape(16, HD)], "vvvv",
        (doc_blocks, partner, recv, rows[1]),
    )
    emb = exchange(emb, "dp")
    dk, dv, *early = main_call(EARLY, where, recv, [rows[k] for k in EARLY], (), (probs,))
    back = dict(zip(EARLY, early))
    for k in EARLY[1:]:
        back[k] = swap(back[k], k)
    n = 4 * n_dp
    heads, part = call(
        gram_part, "va", [shape(GROUP * n, HD), shape(SEQ, n // 2, n, dtype=f32)], "vv", (emb, dk),
    )
    parts = exchange(part, "seq")
    after = (parts,)
    dk, dv, *late = main_call(LATE, where, recv, [rows[k] for k in LATE], (dk, dv), after)
    for k, dq in zip(LATE, late):
        back[k] = swap(dq, k)
    send = call(
        finish, "svvvvvvvvv" + "a" * (len(EARLY) - 1), shape(SEQ, 144, 2 * HD), "v",
        (pack, emb, heads, parts, probs, q_rows, g_rows, recv, dk, dv, *[back[k] for k in EARLY[1:]]),
    )
    recv = exchange(send, "seq")
    dq, dk, dv = call(
        assemble, "sss" + "a" * (SEQ + 1), [shape(BLOCK, DQ), shape(BLOCK, KVH * HD), shape(BLOCK, KVH * HD)], "aaa",
        (*where, recv, *[back[k] for k in range(SEQ)]),
        scratch=[
            pltpu.VMEM((BLOCK, DQ), bf16), pltpu.VMEM((BLOCK, KVH * HD), bf16), pltpu.VMEM((BLOCK, KVH * HD), bf16),
            pltpu.VMEM((SEQ, 16, HD), bf16), pltpu.SemaphoreType.DMA((3 * SEQ + 1,)), pltpu.SemaphoreType.DMA((3,)),
        ],
    )
    return dq[None], dk[None], dv[None]


def solution(mesh):
    rows = P("dp", "seq", None)
    return jax.shard_map(
        functools.partial(on_device, mesh.shape["dp"]),
        mesh=mesh,
        in_specs=(rows, rows, rows, rows, P("dp", None), P("dp", None), P("dp", None)),
        out_specs=(rows, rows, rows),
        check_vma=False,
    )
```

```python
import functools
import math

import jax
import jax.numpy as jnp
from jax import lax
from jax.experimental import pallas as pl
from jax.experimental.pallas import tpu as pltpu
from jax.sharding import PartitionSpec as P

HQ = 32
KVH = 8
HD = 128
BLOCK = 128
DQ = 4096
SEQ = 8
GROUP = HQ // KVH
WIDTH = GROUP * HD
LEN = SEQ * BLOCK
WINDOW = 4
temper = 0.05
eps_mean = 1e-06

ORDER = (1, 4, 5, 2, 3, 6, 7)
NEG = -1e30
LOG2E = math.log2(math.e)
SCALE = HD ** (-0.5)
bf16 = jnp.bfloat16
f32 = jnp.float32
i32 = jnp.int32
HIGHEST = lax.Precision.HIGHEST
LARGE = 60 * 2**20
SMALL = 24 * 2**20

SPACES = {
    "s": pl.BlockSpec(memory_space=pltpu.SMEM),
    "v": pl.BlockSpec(memory_space=pltpu.VMEM),
    "a": pl.BlockSpec(memory_space=pl.ANY),
}


def call(body, ins, out, outs, args, scratch=(), flops=0, limit=SMALL):
    single = not isinstance(out, (list, tuple))
    places = [SPACES[c] for c in outs]
    return pl.pallas_call(
        body,
        out_shape=out,
        in_specs=[SPACES[c] for c in ins],
        out_specs=places[0] if single else places,
        scratch_shapes=list(scratch),
        compiler_params=pltpu.CompilerParams(vmem_limit_bytes=limit),
        cost_estimate=pl.CostEstimate(flops=flops, bytes_accessed=2**20, transcendentals=0),
    )(*args)


def shape(*dims, dtype=bf16):
    return jax.ShapeDtypeStruct(dims, dtype)


def iota(dims, axis):
    return lax.broadcasted_iota(i32, dims, axis)


def dot(a, b, dims, precision=None):
    return lax.dot_general(a, b, ((dims[:1], dims[1:]), ((), ())), precision=precision, preferred_element_type=f32)


def doc_ends(blocks):
    first = blocks[0, 0]
    second = first + blocks[0, 1]
    return first, second, second + blocks[0, 2]


def choose(b, ends, at_first, at_second, at_last):
    return jnp.where(b < ends[0], at_first, jnp.where(b < ends[1], at_second, at_last))


def own_pooled(b, blocks, pad):
    ends = doc_ends(blocks)
    doc = choose(b, ends, 0, 1, 2)
    at = choose(b, ends, *(end * BLOCK - 1 - pad[0, d] for d, end in enumerate(ends))) - b * BLOCK
    here = (at >= 0) & (at < BLOCK)
    return doc, jnp.clip(at, 0, BLOCK - 1), here


def pack_first(me, blocks, pad, k, v, q, g, out, near, q_slab, g_slab, sems, in_sems, out_sem):
    doc, at, here = own_pooled(me[0], blocks, pad)
    base = pl.multiple_of((at >> 4) * 16, 16)
    slabs = (q_slab, g_slab)
    fetch = [pltpu.make_async_copy(far.at[pl.ds(base, 16), :], slabs[i], sems.at[i]) for i, far in enumerate((q, g))]
    for s in range(SEQ):
        for i, far in enumerate((k, v)):
            fetch.append(pltpu.make_async_copy(
                far.at[:, pl.ds(s * HD, HD)], near.at[s, pl.ds(0, BLOCK), pl.ds(i * HD, HD)], in_sems.at[2 * s + i]
            ))
    for copy in fetch:
        copy.start()
    hot = jnp.where((iota((8, 16), 1) == at - base) & here, 1.0, 0.0).astype(bf16)
    row = iota((16, HD), 0)
    for i in range(2):
        fetch[i].wait()
        line = dot(hot, slabs[i][...], (1, 0))[0:1]
        for s in range(SEQ):
            rows = jnp.zeros((16, HD), f32)
            for h in range(GROUP):
                piece = line[:, s * WIDTH + h * HD:s * WIDTH + (h + 1) * HD]
                rows = jnp.where(row == h * 4 + doc, piece, rows)
            near[s, 128:144, i * HD:(i + 1) * HD] = rows.astype(bf16)
    for copy in fetch[2:]:
        copy.wait()
    back = pltpu.make_async_copy(near, out, out_sem.at[0])
    back.start()
    back.wait()


def pack_rest(me, q, g, _, *refs):
    outs, stage, in_sems, out_sems = refs[:SEQ], refs[SEQ], refs[SEQ + 1], refs[SEQ + 2]
    arriving, leaving = [], []
    for k in (*ORDER, 0):
        at = pl.ds(pl.multiple_of((me[0] ^ k) * WIDTH, WIDTH), WIDTH)
        arriving.append((
            pltpu.make_async_copy(q.at[:, at], stage.at[k, :, pl.ds(0, WIDTH)], in_sems.at[2 * k]),
            pltpu.make_async_copy(g.at[:, at], stage.at[k, :, pl.ds(WIDTH, WIDTH)], in_sems.at[2 * k + 1]),
        ))
        leaving.append(pltpu.make_async_copy(stage.at[k], outs[k], out_sems.at[k]))
    for pair in arriving:
        for copy in pair:
            copy.start()
    for pair, copy in zip(arriving, leaving):
        for one in pair:
            one.wait()
        copy.start()
    for copy in leaving:
        copy.wait()


def pooled_forward(blocks, partner, recv, _, emb, probs, q_rows, g_rows):
    both = jnp.zeros((16, 2 * HD), f32)
    for s in range(SEQ):
        both = both + recv[s, 128:144, :].astype(f32)
    q_low = both[:, 0:HD].astype(bf16)
    q_rows[...] = q_low
    g_rows[...] = both[:, HD:2 * HD].astype(bf16)
    keys = jnp.concatenate([recv[s, 0:128, 0:128] for s in range(SEQ)], axis=0)
    vals = jnp.concatenate([recv[s, 0:128, 128:256] for s in range(SEQ)], axis=0)
    first, second, last = doc_ends(blocks)
    doc = iota((16, LEN), 0) & 3
    block = iota((16, LEN), 1) >> 7
    low = jnp.where(doc == 0, 0, jnp.where(doc == 1, first, second))
    high = jnp.where(doc == 0, first, jnp.where(doc == 1, second, last))
    scores = dot(q_low, keys, (1, 1)) * (SCALE * LOG2E)
    scores = jnp.where((block >= low) & (block < high), scores, NEG)
    peak = jnp.max(scores, axis=1, keepdims=True)
    weights = jnp.exp2(scores - peak)
    p = weights / jnp.sum(weights, axis=1, keepdims=True)
    probs[...] = p
    rows = dot(p.astype(bf16), vals, (1, 0)).astype(bf16).astype(f32)
    row, lane = iota((16, HD), 0), iota((16, HD), 1)
    rows = jnp.where((row & 3) < 3, rows, 0.0)
    for d in range(3):
        index = partner[0, d]
        spot = (lax.div(index, 3) * 4 + lax.rem(index, 3)).astype(f32)
        rows = jnp.where((row == 3) & (lane == d), spot, rows)
    rows = rows.astype(bf16)
    for copy in range(emb.shape[0]):
        emb[copy] = rows


def gram_part(rows, _, heads, part):
    packs = rows.shape[0]
    n = packs * 4
    flat = rows[...].reshape(packs * 16, HD)
    r, c = iota((4 * n, packs * 16), 0), iota((4 * n, packs * 16), 1)
    i, h = r & (n - 1), r // n
    hit = (c == (i >> 2) * 16 + h * 4 + (i & 3)) & ((i & 3) < 3)
    mixed = dot(jnp.where(hit, 1.0, 0.0).astype(bf16), flat, (1, 0)).astype(bf16)
    heads[...] = mixed
    total = jnp.zeros((n, n), f32)
    for h in range(GROUP):
        e = mixed[h * n:(h + 1) * n]
        total = total + dot(e, e, (1, 1))
    half = n // 2
    row, col = iota((n, n), 0), iota((n, n), 1)
    diagonal = jnp.sum(jnp.where(row == col, total, 0.0), axis=0, keepdims=True)
    row, col = iota((half, n), 0), iota((half, n), 1)
    turned = pltpu.roll(total[half:], half, 1)
    packed = jnp.where(row >= col, total[:half], turned)
    packed = jnp.where(col >= half, jnp.where(row == 3, diagonal, total[:half]), packed)
    for s in range(SEQ):
        part[s] = packed


def unpack_gram(packed):
    half, n = packed.shape
    row, col = iota((n, n), 0), iota((n, n), 1)
    tall = jnp.concatenate([packed, packed], axis=0)
    turned = pltpu.roll(tall, half, 1)
    upper = (row < half) & (((col < half) & (row > col)) | ((col >= half) & (row != 3)))
    lower = (row >= half) & (row < col)
    one = jnp.where(upper, tall, 0.0) + jnp.where(lower, turned, 0.0)
    diagonal = jnp.where(row < half, tall, packed[3:4])
    return one + one.T + jnp.where(row == col, diagonal, 0.0)


def attend(me, blocks, pad, steps, recv, rows, dk, dv, outs):
    ends = doc_ends(blocks)
    for k, row, out in zip(steps, rows, outs):
        b = me[0] ^ k
        low = choose(b, ends, 0, ends[0], ends[1])
        high = choose(b, ends, *ends)
        _, spot, here = own_pooled(b, blocks, pad)
        start = jnp.minimum(low, SEQ - WINDOW)
        keys = jnp.concatenate([recv[start + j, 0:128, 0:128] for j in range(WINDOW)], axis=0)
        vals = jnp.concatenate([recv[start + j, 0:128, 128:256] for j in range(WINDOW)], axis=0)
        q = jnp.concatenate([row[:, h * HD:(h + 1) * HD] for h in range(GROUP)], axis=0)
        g = jnp.concatenate([row[:, WIDTH + h * HD:WIDTH + (h + 1) * HD] for h in range(GROUP)], axis=0)
        pooled = ((iota((GROUP * BLOCK, HD), 0) & (BLOCK - 1)) == spot) & here
        g = jnp.where(pooled, 0.0, g.astype(f32)).astype(bf16)
        dscores, probs_low = [], []
        for at in range(0, WIDTH, 2 * HD):
            scores = dot(keys, q[at:at + 2 * HD], (1, 1)) * (SCALE * LOG2E)
            parts = []
            for j in range(WINDOW):
                seen = (start + j >= low) & (start + j < high)
                parts.append(scores[j * BLOCK:(j + 1) * BLOCK] + jnp.where(seen, 0.0, NEG))
            scores = jnp.concatenate(parts, axis=0)
            peak = jnp.max(scores, axis=0, keepdims=True)
            weights = jnp.exp2(scores - peak)
            probs = weights * (1.0 / jnp.sum(weights, axis=0, keepdims=True))
            dprob = dot(vals, g[at:at + 2 * HD], (1, 1))
            delta = jnp.sum(probs * dprob, axis=0, keepdims=True)
            dscores.append((probs * (dprob - delta)).astype(bf16))
            probs_low.append(probs.astype(bf16))
        dscore = jnp.concatenate(dscores, axis=1)
        dq = dot(dscore, keys, (0, 0)) * SCALE
        for h in range(GROUP):
            out[0:BLOCK, h * HD:(h + 1) * HD] = dq[h * BLOCK:(h + 1) * BLOCK].astype(bf16)
        dk_add = dot(dscore, q, (1, 0))
        dv_add = dot(jnp.concatenate(probs_low, axis=1), g, (1, 0))
        for j in range(WINDOW):
            dk[start + j] += dk_add[j * BLOCK:(j + 1) * BLOCK]
            dv[start + j] += dv_add[j * BLOCK:(j + 1) * BLOCK]


EARLY = (0, 1, 4, 5)
LATE = (2, 3, 6, 7)


def main_early(me, blocks, pad, recv, *refs):
    n = len(EARLY)
    dk, dv, outs, sums = refs[-4 - n], refs[-3 - n], refs[-2 - n:-2], refs[-2:]
    for total in sums:
        total[...] = jnp.zeros_like(total)
    attend(me, blocks, pad, EARLY, recv, refs[:n], *sums, outs)
    dk[...] = sums[0][...].astype(bf16)
    dv[...] = sums[1][...].astype(bf16)


def main_late(pack, me, blocks, pad, raw, heads, parts, probs, q_rows, g_rows, recv, dk, dv, *refs):
    n = len(LATE)
    rows, outs, sums = refs[:n], refs[n:n + SEQ], refs[n + SEQ:]
    sums[0][...] = dk[...].astype(f32)
    sums[1][...] = dv[...].astype(f32)
    attend(me, blocks, pad, LATE, recv, rows, *sums, [outs[k] for k in LATE])
    finish(me, pack, raw, heads, parts, probs, q_rows, g_rows, recv, *sums, outs)


def finish(me, pack, raw, heads, parts, probs_ref, q_rows, g_rows, recv, dk, dv, outs):
    packs = raw.shape[0]
    n = packs * 4
    gram = parts[0]
    for s in range(1, SEQ):
        gram = gram + parts[s]
    gram = unpack_gram(gram)
    row, col = iota((n, n), 0), iota((n, n), 1)
    flat = raw[...].reshape(packs * 16, HD)
    r, c = iota((n, packs * 16), 0), iota((n, packs * 16), 1)
    hit = jnp.where(c == (r >> 2) * 16 + 3, 1.0, 0.0).astype(bf16)
    spots = dot(hit, flat, (1, 0))
    r, c = iota((n, HD), 0), iota((n, HD), 1)
    partner = jnp.sum(jnp.where(c == (r & 3), spots, 0.0), axis=1, keepdims=True)
    real_row, real_col = (row & 3) < 3, (col & 3) < 3
    chosen = jnp.where((partner.astype(i32) == col) & real_row, 1.0, 0.0)
    squares = jnp.where(row == col, gram, 0.0)
    square_row = jnp.sum(squares, axis=1, keepdims=True)
    square_col = jnp.sum(squares, axis=0, keepdims=True)
    scale_row = lax.rsqrt(square_row / DQ + eps_mean)
    scale_col = lax.rsqrt(square_col / DQ + eps_mean)
    sim = gram * scale_row * scale_col / (DQ * temper)
    weight = jnp.where((row != col) & real_row & real_col, jnp.exp(sim - 1.0 / temper), 0.0)
    total = jnp.sum(weight, axis=1, keepdims=True)
    attract = weight / jnp.where((iota((n, 1), 0) & 3) < 3, total, 1.0) - chosen
    terms = (attract + attract.T) * scale_col
    inner = jnp.sum(terms * gram, axis=1, keepdims=True)
    own = jnp.where(row == col, scale_row * scale_row * inner / DQ, 0.0)
    mix = scale_row / (DQ * temper) * (terms - own)
    r, c = iota((16, n), 0), iota((16, n), 1)
    pick = jnp.where((c == pack[0] * 4 + (r & 3)) & ((r & 3) < 3), 1.0, 0.0)
    mix = dot(pick, mix, (1, 0), HIGHEST)
    grad = jnp.zeros((16, HD), f32)
    r = iota((16, HD), 0)
    for h in range(GROUP):
        grad = jnp.where((r >> 2) == h, dot(mix, heads[h * n:(h + 1) * n].astype(f32), (1, 0), HIGHEST), grad)
    g = (g_rows[...].astype(f32) + grad).astype(bf16)

    keys = jnp.concatenate([recv[s, 0:128, 0:128] for s in range(SEQ)], axis=0)
    vals = jnp.concatenate([recv[s, 0:128, 128:256] for s in range(SEQ)], axis=0)
    probs = probs_ref[...]
    dprob = dot(g, vals, (1, 1))
    delta = jnp.sum(probs * dprob, axis=1, keepdims=True)
    dscore = (probs * (dprob - delta)).astype(bf16)
    dq = (dot(dscore, keys, (1, 0)) * SCALE).astype(bf16)
    dk_add = dot(dscore, q_rows[...], (0, 0))
    dv_add = dot(probs.astype(bf16), g, (0, 0))
    for s in range(SEQ):
        at = slice(s * BLOCK, (s + 1) * BLOCK)
        dk[s] = (dk[s] + dk_add[at]) * SCALE
        dv[s] = dv[s] + dv_add[at]
    for k in range(SEQ):
        out = outs[k]
        at = out.shape[1] - 2 * HD
        out[0:BLOCK, at:at + HD] = dk[me[0] ^ k].astype(bf16)
        out[0:BLOCK, at + HD:] = dv[me[0] ^ k].astype(bf16)
        for lane in range(0, out.shape[1], HD):
            out[BLOCK:, lane:lane + HD] = dq


def assemble(me, blocks, pad, *refs):
    n = len(EARLY)
    early, rows, outs = refs[:n], refs[n:n + SEQ], refs[n + SEQ:n + SEQ + 3]
    dq, dk, dv, fixes, in_sems, out_sems = refs[n + SEQ + 3:]
    near = (dq, dk, dv)
    doc, at, here = own_pooled(me[0], blocks, pad)
    base = pl.multiple_of((at >> 4) * 16, 16)
    fetch, later = [], []
    for k in range(SEQ):
        s = me[0] ^ k
        lanes = pl.ds(pl.multiple_of(s * WIDTH, WIDTH), WIDTH)
        left = rows[k].shape[1] - 2 * HD
        source = early[EARLY.index(k)] if k in EARLY else rows[k].at[pl.ds(0, BLOCK), pl.ds(0, WIDTH)]
        fetch.append(pltpu.make_async_copy(source, dq.at[:, lanes], in_sems.at[4 * k]))
        fetch.append(pltpu.make_async_copy(
            rows[k].at[pl.ds(BLOCK, 16), pl.ds(left, HD)], fixes.at[k], in_sems.at[4 * k + 1]
        ))
        lanes = pl.ds(pl.multiple_of(s * HD, HD), HD)
        for i, to in enumerate((dk, dv)):
            later.append(pltpu.make_async_copy(
                rows[k].at[pl.ds(0, BLOCK), pl.ds(left + i * HD, HD)], to.at[:, lanes], in_sems.at[4 * k + 2 + i]
            ))
    sends = [pltpu.make_async_copy(near[i], outs[i], out_sems.at[i]) for i in range(3)]
    for copy in (*fetch, *later):
        copy.start()
    for copy in fetch:
        copy.wait()

    @pl.when(here)
    def _():
        row = iota((16, HD), 0)
        for k in range(SEQ):
            fixed = fixes[k].astype(f32)
            for h in range(GROUP):
                line = jnp.sum(jnp.where(row == h * 4 + doc, fixed, 0.0), axis=0, keepdims=True)
                lanes = pl.ds(pl.multiple_of((me[0] ^ k) * WIDTH + h * HD, HD), HD)
                slab = dq[pl.ds(base, 16), lanes].astype(f32)
                dq[pl.ds(base, 16), lanes] = jnp.where(row == at - base, line, slab).astype(bf16)

    sends[0].start()
    for copy in later:
        copy.wait()
    for send in sends[1:]:
        send.start()
    for send in sends:
        send.wait()


def exchange(x, axis, **kw):
    return lax.all_to_all(x, axis, split_axis=0, concat_axis=0, tiled=True, **kw)


def swap(x, k):
    return lax.ppermute(x, "seq", [(s, s ^ k) for s in range(SEQ)])


def on_device(n_dp, queries, keys, values, out_grad, doc_blocks, pad_count, partner):
    me = lax.axis_index("seq").astype(i32).reshape(1)
    pack = lax.axis_index("dp").astype(i32).reshape(1)
    where = (me, doc_blocks, pad_count)
    q, k, v, g = queries[0], keys[0], values[0], out_grad[0]
    pair = pltpu.SemaphoreType.DMA((2,))
    one = pltpu.SemaphoreType.DMA((1,))
    each = pltpu.SemaphoreType.DMA((SEQ,))
    double = pltpu.SemaphoreType.DMA((2 * SEQ,))
    send = call(
        pack_first, "sssaaaa", shape(SEQ, 144, 256), "a", (*where, k, v, q, g),
        scratch=[
            pltpu.VMEM((SEQ, 144, 256), bf16), pltpu.VMEM((16, DQ), bf16), pltpu.VMEM((16, DQ), bf16), pair, double, one,
        ],
        limit=LARGE,
    )
    recv = exchange(send, "seq")
    mine = call(
        pack_rest, "saaa", [shape(BLOCK, 2 * WIDTH)] * SEQ, "a" * SEQ, (me, q, g, send),
        scratch=[pltpu.VMEM((SEQ, BLOCK, 2 * WIDTH), bf16), double, each], limit=LARGE,
    )
    rows = [mine[0]] + [None] * (SEQ - 1)
    for step in ORDER:
        rows[step] = swap(mine[step], step)

    emb, probs, q_rows, g_rows = call(
        pooled_forward, "ssva",
        [shape(n_dp, 16, HD), shape(16, LEN, dtype=f32), shape(16, HD), shape(16, HD)], "vvvv",
        (doc_blocks, partner, recv, rows[1]),
    )
    emb = exchange(emb, "dp")
    total = shape(SEQ, BLOCK, HD)
    block = shape(BLOCK, WIDTH)
    sums = [pltpu.VMEM(total.shape, f32), pltpu.VMEM(total.shape, f32)]
    dk, dv, *early = call(
        main_early, "sssv" + "v" * len(EARLY) + "a", [total, total] + [block] * len(EARLY), "vv" + "v" * len(EARLY),
        (*where, recv, *[rows[k] for k in EARLY], probs), scratch=sums, flops=6 * 10**9,
    )
    back = {k: swap(dq, k) if k else dq for k, dq in zip(EARLY, early)}
    n = 4 * n_dp
    heads, part = call(
        gram_part, "va", [shape(GROUP * n, HD), shape(SEQ, n // 2, n, dtype=f32)], "vv", (emb, dk),
    )
    parts = exchange(part, "seq")
    sends = call(
        main_late, "ssss" + "v" * (9 + len(LATE)),
        [shape(BLOCK + 16, (WIDTH if k in LATE else 0) + 2 * HD) for k in range(SEQ)], "v" * SEQ,
        (pack, *where, emb, heads, parts, probs, q_rows, g_rows, recv, dk, dv, *[rows[k] for k in LATE]), scratch=sums,
        flops=6 * 10**9,
    )
    held = lax.optimization_barrier((*sends, *[back[k] for k in EARLY[1:]]))
    sends = held[:SEQ]
    back.update(zip(EARLY[1:], held[SEQ:]))
    last = [swap(sends[k], k) if k else sends[k] for k in range(SEQ)]
    dq, dk, dv = call(
        assemble, "sss" + "a" * (SEQ + len(EARLY)), [shape(BLOCK, DQ), shape(BLOCK, KVH * HD), shape(BLOCK, KVH * HD)],
        "aaa", (*where, *[back[k] for k in EARLY], *last),
        scratch=[
            pltpu.VMEM((BLOCK, DQ), bf16), pltpu.VMEM((BLOCK, KVH * HD), bf16), pltpu.VMEM((BLOCK, KVH * HD), bf16),
            pltpu.VMEM((SEQ, 16, HD), bf16), pltpu.SemaphoreType.DMA((4 * SEQ,)), pltpu.SemaphoreType.DMA((3,)),
        ],
    )
    return dq[None], dk[None], dv[None]


def solution(mesh):
    rows = P("dp", "seq", None)
    return jax.shard_map(
        functools.partial(on_device, mesh.shape["dp"]),
        mesh=mesh,
        in_specs=(rows, rows, rows, rows, P("dp", None), P("dp", None), P("dp", None)),
        out_specs=(rows, rows, rows),
        check_vma=False,
    )
```
